256 devices in a mesh: rep: 32 (over z, x_hi, core), tp: 8 (over x_lo, y).
Axes of the slice: x: 4 (x_hi: 2, x_lo: 2; x = x_hi * 2 + x_lo), y: 4, z: 8, core: 2. Of those that a mesh axis runs over, the one named last changes fastest.
Arguments:
- inputs: bfloat16 [6144, 2560], P(('rep', 'tp')), may hold values from -6 to 6
- cotangent: bfloat16 [6144, 2560], P(('rep', 'tp')), may hold values from -6 to 6
- gate_weight: bfloat16 [32, 2560, 2048], P('rep', None, 'tp'), may hold values from -0.125 to 0.125
- up_weight: bfloat16 [32, 2560, 2048], P('rep', None, 'tp'), may hold values from -0.125 to 0.125
- down_weight: bfloat16 [32, 2048, 2560], P('rep', 'tp'), may hold values from -0.0625 to 0.0625
- gate_moment: bfloat16 [32, 2560, 2048], P('rep', None, 'tp'), may hold values from -48 to 48
- up_moment: bfloat16 [32, 2560, 2048], P('rep', None, 'tp'), may hold values from -48 to 48
- down_moment: bfloat16 [32, 2048, 2560], P('rep', 'tp'), may hold values from -48 to 48
- step_count: int32 [], replicated, may hold values from 0 to 999
Outputs:
- block_out: bfloat16 [6144, 2560], P(('rep', 'tp'))
- input_grad: bfloat16 [6144, 2560], P(('rep', 'tp'))
- new_gate: bfloat16 [32, 2560, 2048], P('rep', None, 'tp')
- new_up: bfloat16 [32, 2560, 2048], P('rep', None, 'tp')
- new_down: bfloat16 [32, 2048, 2560], P('rep', 'tp')
The draws below stay inside these ranges and needn't reach their ends.
All inputs are finite; a program needn't handle non-finite values.
Results may differ from the reference program's by a relative error of at most 0.0058.
Values may be sent and summed in bfloat16 or wider, within the bound.
A program may use at most 128 MiB of HBM per device.

```python
import jax
import jax.numpy as jnp
from jax import lax

D = 2560
FF = 8192
SPLIT = 4
TOK_DEV = 768
TOKENS = 6144
N_REP = 32


def block_levels(key, dims, cuts, smallest, top_value):
    gain, own = 1.0, jax.random.fold_in(key, 6)
    for axis_at, blocks in cuts:
        draws = jnp.exp(jax.random.uniform(jax.random.fold_in(own, axis_at), (blocks,), jnp.float32, smallest / len(cuts), top_value / len(cuts)))
        gain = gain * jnp.repeat(draws, dims[axis_at] // blocks).reshape([-1 if axis == axis_at else 1 for axis in range(len(dims))])
    return gain


def bell_draw(own_key, extent, width, bound, cuts=(), held_as=jnp.bfloat16):
    level = block_levels(own_key, extent, cuts, -0.22, 0.18) if cuts else 1.0
    array = jax.random.normal(own_key, extent, jnp.float32) * width * level
    return jnp.minimum(jnp.maximum(array, -bound), bound).astype(held_as)


def setup_inputs(seed: int = 0) -> dict:
    splits = jax.random.split(jax.random.key(seed), 10)
    inputs = bell_draw(splits[0], (TOKENS, D), 1.0, 6.0, ((0, 256),))
    cotangent = bell_draw(splits[1], (TOKENS, D), 1.0, 6.0, ((0, 256),))
    gate_weight = bell_draw(splits[2], (N_REP, D, FF // SPLIT), D ** -0.5, 0.125, ((0, 32), (2, 8)))
    up_weight = bell_draw(splits[3], (N_REP, D, FF // SPLIT), D ** -0.5, 0.125, ((0, 32), (2, 8)))
    down_weight = bell_draw(splits[4], (N_REP, FF // SPLIT, D), FF ** -0.5, 0.0625, ((0, 32), (1, 8)))
    gate_moment = bell_draw(splits[5], (N_REP, D, FF // SPLIT), 8.0, 48.0, ((0, 32), (2, 8)))
    up_moment = bell_draw(splits[6], (N_REP, D, FF // SPLIT), 8.0, 48.0, ((0, 32), (2, 8)))
    down_moment = bell_draw(splits[7], (N_REP, FF // SPLIT, D), 8.0, 48.0, ((0, 32), (1, 8)))
    step_count = jax.random.randint(splits[8], (), 0, 1000).astype(jnp.int32)
    return {"inputs": inputs, "cotangent": cotangent, "gate_weight": gate_weight, "up_weight": up_weight, "down_weight": down_weight, "gate_moment": gate_moment, "up_moment": up_moment, "down_moment": down_moment, "step_count": step_count}


MOMENT = 0.9
LEARN = 0.001


def join_columns(blocks):
    return jnp.transpose(blocks, (1, 0, 2)).reshape(D, FF)


def split_columns(matrix):
    return jnp.transpose(matrix.reshape(D, SPLIT, FF // SPLIT), (1, 0, 2))


def advance(weight, moment, grad):
    return (weight.astype(jnp.float32) - LEARN * (MOMENT * moment.astype(jnp.float32) + grad)).astype(jnp.bfloat16)


def one_replica(pieces):
    x, g, wg_blocks, wu_blocks, wd_blocks, mg_blocks, mu_blocks, md_blocks = pieces
    wg = join_columns(wg_blocks)
    wu = join_columns(wu_blocks)
    mg = join_columns(mg_blocks)
    mu = join_columns(mu_blocks)
    wd = wd_blocks.reshape(FF, D)
    md = md_blocks.reshape(FF, D)
    gate = jnp.dot(x, wg, preferred_element_type=jnp.float32)
    up = jnp.dot(x, wu, preferred_element_type=jnp.float32)
    sig = jax.nn.sigmoid(gate)
    silu_gate = gate * sig
    act = (silu_gate * up).astype(jnp.bfloat16)
    out = (x.astype(jnp.float32) + jnp.dot(act, wd, preferred_element_type=jnp.float32)).astype(jnp.bfloat16)
    down_grad = jnp.dot(act.T, g, preferred_element_type=jnp.float32)
    act_grad = jnp.dot(g, wd.T, preferred_element_type=jnp.float32)
    gate_back = (act_grad * up * sig * (1.0 + gate * (1.0 - sig))).astype(jnp.bfloat16)
    up_back = (act_grad * silu_gate).astype(jnp.bfloat16)
    gate_grad = jnp.dot(x.T, gate_back, preferred_element_type=jnp.float32)
    up_grad = jnp.dot(x.T, up_back, preferred_element_type=jnp.float32)
    back_sum = jnp.dot(gate_back, wg.T, preferred_element_type=jnp.float32) + jnp.dot(up_back, wu.T, preferred_element_type=jnp.float32)
    back = (g.astype(jnp.float32) + back_sum).astype(jnp.bfloat16)
    half_gate = split_columns(advance(wg, mg, gate_grad))
    half_up = split_columns(advance(wu, mu, up_grad))
    half_down = advance(wd, md, down_grad).reshape(SPLIT, FF // SPLIT, D)
    return out, back, half_gate, half_up, half_down


def mean_pair(half, partner):
    return ((half.astype(jnp.float32) + half[partner].astype(jnp.float32)) * 0.5).astype(jnp.bfloat16)


def reference(inputs, cotangent, gate_weight, up_weight, down_weight, gate_moment, up_moment, down_moment, step_count):
    count = N_REP // SPLIT
    xs = inputs.reshape(count, TOK_DEV, D)
    gs = cotangent.reshape(count, TOK_DEV, D)
    wgs = gate_weight.reshape(count, SPLIT, D, FF // SPLIT)
    wus = up_weight.reshape(count, SPLIT, D, FF // SPLIT)
    wds = down_weight.reshape(count, SPLIT, FF // SPLIT, D)
    mgs = gate_moment.reshape(count, SPLIT, D, FF // SPLIT)
    mus = up_moment.reshape(count, SPLIT, D, FF // SPLIT)
    mds = down_moment.reshape(count, SPLIT, FF // SPLIT, D)
    out, back, half_gate, half_up, half_down = lax.map(one_replica, (xs, gs, wgs, wus, wds, mgs, mus, mds))
    levels = count.bit_length() - 1
    level = jnp.mod(step_count, levels).astype(jnp.int32)
    partner = jnp.bitwise_xor(jnp.arange(count, dtype=jnp.int32), jnp.left_shift(jnp.int32(1), level))
    new_gate = mean_pair(half_gate, partner).reshape(N_REP, D, FF // SPLIT)
    new_up = mean_pair(half_up, partner).reshape(N_REP, D, FF // SPLIT)
    new_down = mean_pair(half_down, partner).reshape(N_REP, FF // SPLIT, D)
    return out.reshape(TOKENS, D), back.reshape(TOKENS, D), new_gate, new_up, new_down
```

```python
import functools

import jax
import jax.numpy as jnp
from jax import lax
from jax.experimental import pallas as pl
from jax.experimental.pallas import tpu as pltpu
from jax.sharding import PartitionSpec as P

MESH = pl.DeviceIdType.MESH
SPLIT = 4
SIDE = 4
MOMENT = 0.9
LEARN = 0.001
CHUNK = 512
F32 = jnp.float32
BF16 = jnp.bfloat16


def at_multiple(index, of):
    return pl.multiple_of(index, of)


def kernel(
    level,
    x_in,
    g_in,
    wg_in,
    wu_in,
    wd_in,
    mg_in,
    mu_in,
    md_in,
    out_o,
    gin_o,
    ng_o,
    nu_o,
    nd_o,
    x3,
    g3,
    xc,
    gc,
    wg,
    wu,
    wd,
    mg,
    mu,
    md,
    rg,
    ru,
    rd,
    gate,
    up,
    act,
    gb,
    ub,
    actt,
    sx,
    sg,
    px,
    pg,
    load_sem,
    own_sem,
    wave_send,
    wave_recv,
    pair_send,
    pair_recv,
    sum_send,
    sum_recv,
    gossip_send,
    gossip_recv,
    write_sem,
):
    rows, depth = x_in.shape
    width = wg.shape[1]
    blocks = SIDE * SIDE
    half = blocks * rows
    r, t = lax.axis_index("rep"), lax.axis_index("tp")
    z, core = r // SPLIT, r % 2
    x, y = (r // 2) % 2 * 2 + t // SIDE, t % SIDE
    s = x + core * (y - x)
    f = y + core * (x - y)

    def turn(index):
        return (index + SIDE) % SIDE

    def device(cc, ss, ff, zz=None):
        xx = ss + cc * (ff - ss)
        yy = ff + cc * (ss - ff)
        return ((z if zz is None else zz) * SPLIT + xx // 2 * 2 + cc, xx % 2 * SIDE + yy)

    f_plus, f_minus = device(core, s, turn(f + 1)), device(core, s, turn(f - 1))
    s_plus, s_minus = device(core, turn(s + 1), f), device(core, turn(s - 1), f)
    sibling = (z * SPLIT + x // 2 * 2 + 1 - core, t)
    step = 2**level
    partner_z = z + step - 2 * step * (z // step % 2)
    partner = device(core, s, f, partner_z)
    peers = [device(core, turn(s + k // SIDE), turn(f + k % SIDE)) for k in range(1, blocks)]

    def remote(src, dst, send, recv, to):
        return pltpu.make_async_remote_copy(
            src_ref=src, dst_ref=dst, send_sem=send, recv_sem=recv, device_id=to, device_id_type=MESH
        )

    loads = [
        pltpu.make_async_copy(src.at[0], dst, load_sem.at[i])
        for i, (src, dst) in enumerate(
            ((wg_in, wg), (wu_in, wu), (wd_in, wd), (md_in, md), (mg_in, mg), (mu_in, mu))
        )
    ]

    sent = []
    waves = [(x_in, x3, 0, depth)] + [(g_in, g3, col, CHUNK) for col in range(0, depth, CHUNK)]
    own_copies = [
        pltpu.make_async_copy(
            src.at[:, pl.ds(col, wide)],
            land.at[core * blocks + s * SIDE + f, :, pl.ds(col, wide)],
            own_sem.at[w],
        )
        for w, (src, land, col, wide) in enumerate(waves)
    ]

    class Wave:
        def __init__(self, w):
            self.w = w
            self.src, self.land, self.col, self.wide = waves[w]
            self.sends = 0

        def cols(self, part):
            wide = self.wide
            if part == "all":
                return pl.ds(self.col, wide)
            return pl.ds(self.col + (wide // 2 if part == "high" else 0), wide // 2)

        def block(self, ds, df, part="all"):
            at = core * blocks + turn(s + ds) * SIDE + turn(f + df)
            return self.land.at[at, :, self.cols(part)]

        def group(self, ds, part="all", other=False):
            if other:
                at = (1 - core) * blocks + turn(f + ds) * SIDE
            else:
                at = core * blocks + turn(s + ds) * SIDE
            return self.land.at[pl.ds(at, SIDE), :, self.cols(part)]

        def send(self, src, dst, slot, to):
            copy = remote(
                src, dst, wave_send.at[self.w, self.sends], wave_recv.at[self.w, slot], to
            )
            self.sends += 1
            copy.start()
            sent.append(copy)

        def wait(self, dst, slot):
            remote(
                dst, dst, wave_send.at[self.w, 0], wave_recv.at[self.w, slot], sibling
            ).wait_recv()

        def start(self):
            mine = self.src.at[:, self.cols("all")]
            to = self.block(0, 0)
            self.send(mine, to, 0, f_plus)
            self.send(mine, to, 1, f_minus)
            own_copies[self.w].start()

        def near(self):
            self.wait(self.block(0, -1), 0)
            self.wait(self.block(0, 1), 1)
            for df, part, slot, to in ((-1, "low", 2, f_plus), (1, "high", 3, f_minus)):
                ref = self.block(0, df, part)
                self.send(ref, ref, slot, to)

        def far(self):
            self.wait(self.block(0, 2, "low"), 2)
            self.wait(self.block(0, 2, "high"), 3)

        def to_sibling(self, ds, slot):
            ref = self.group(ds)
            self.send(ref, ref, 20 + slot, sibling)

        def spread(self):
            self.far()
            own_copies[self.w].wait()
            ref = self.group(0)
            self.send(ref, ref, 4, s_plus)
            self.send(ref, ref, 8, s_minus)
            self.to_sibling(0, 0)

        def onward(self):
            for ds, part, slot, to in ((-1, "low", 4, s_plus), (1, "high", 8, s_minus)):
                self.wait(self.group(ds), slot)
                ref = self.group(ds, part)
                self.send(ref, ref, slot + 8, to)
            self.to_sibling(-1, 1)
            self.to_sibling(1, 2)

        def last(self):
            self.wait(self.group(2, "low"), 12)
            self.wait(self.group(2, "high"), 16)
            self.to_sibling(2, 3)

        def other(self):
            for slot, ds in enumerate((0, -1, 1, 2)):
                self.wait(self.group(ds, other=True), 20 + slot)

        def spread_block(self, df, src=None):
            ref = self.block(0, df)
            src = ref if src is None else src
            self.send(src, ref, 4 + df % SIDE, s_plus)
            self.send(src, ref, 8 + df % SIDE, s_minus)

        def onward_block(self, df):
            for ds, part, slot, to in ((-1, "low", 4, s_plus), (1, "high", 8, s_minus)):
                self.wait(self.block(ds, df), slot + df % SIDE)
                ref = self.block(ds, df, part)
                self.send(ref, ref, slot + 8 + df % SIDE, to)

        def last_block(self, df):
            self.wait(self.block(2, df, "low"), 12 + df % SIDE)
            self.wait(self.block(2, df, "high"), 16 + df % SIDE)

    def repack(land, flat, which, col, wide):
        def body(i, carry):
            b = which * blocks + 2 * i
            pair = jnp.concatenate(
                [
                    land[b, :, pl.ds(col, wide)].astype(F32),
                    land[b + 1, :, pl.ds(col, wide)].astype(F32),
                ],
                0,
            )
            flat[pl.ds(at_multiple(b * rows, 2 * rows), 2 * rows), pl.ds(col, wide)] = pair.astype(
                BF16
            )
            return carry

        lax.fori_loop(0, blocks // 2, body, 0)

    def forward(which):
        at = pl.ds(at_multiple(which * half, half), half)
        tokens = xc[at, :]
        g_val = jnp.dot(tokens, wg[...], preferred_element_type=F32)
        gate[at, :] = g_val
        u_val = jnp.dot(tokens, wu[...], preferred_element_type=F32)
        up[at, :] = u_val
        act[at, :] = (g_val * jax.nn.sigmoid(g_val) * u_val).astype(BF16)

    def advance(weight, moment, grad):
        total = MOMENT * moment.astype(F32) + grad
        return (weight.astype(F32) - LEARN * total).astype(BF16)

    pieces = depth // CHUNK

    def gossip(kind, piece):
        at = pl.ds(piece * CHUNK, CHUNK)
        mine, theirs = ((md, rd), (mg, rg), (mu, ru))[kind]
        index = (slice(None), at) if kind == 0 else (at, slice(None))
        n = kind * pieces + piece
        return remote(
            mine.at[index], theirs.at[index], gossip_send.at[n], gossip_recv.at[n], partner
        )

    def down(piece):
        at = pl.ds(piece * CHUNK, CHUNK)
        grad = jnp.dot(actt[...], gc[:, at], preferred_element_type=F32)
        md[:, at] = advance(wd[:, at], md[:, at], grad)
        gossip(0, piece).start()

    for load in loads:
        load.start()
    barrier = pltpu.get_barrier_semaphore()
    for to in peers + [sibling, partner]:
        pl.semaphore_signal(barrier, inc=1, device_id=to, device_id_type=MESH)
    pl.semaphore_wait(barrier, len(peers) + 2)

    wave = [Wave(w) for w in range(len(waves))]
    first, g_waves = wave[0], wave[1:]
    first.start()
    first.spread_block(0, x_in.at[:, pl.ds(0, depth)])
    first.near()
    first.spread_block(-1)
    first.spread_block(1)
    first.onward_block(0)
    first.far()
    first.spread_block(2)
    own_copies[0].wait()
    first.to_sibling(0, 0)
    first.onward_block(-1)
    first.onward_block(1)
    for one in g_waves:
        one.start()
    first.onward_block(2)
    first.to_sibling(-1, 1)
    first.to_sibling(1, 2)
    for one in g_waves:
        one.near()
    g_waves[0].spread()
    g_waves[1].spread()
    for df in (0, -1, 1, 2):
        first.last_block(df)
    first.to_sibling(2, 3)
    repack(x3, xc, core, 0, depth)
    loads[0].wait()
    loads[1].wait()
    g_waves[0].onward()
    forward(core)
    g_waves[2].spread()
    first.other()
    repack(x3, xc, 1 - core, 0, depth)
    g_waves[0].last()
    g_waves[1].onward()
    forward(1 - core)
    g_waves[3].spread()
    actt[...] = act[...].T
    loads[2].wait()
    loads[3].wait()
    n = len(g_waves)
    for w in range(n):
        g_waves[w].other()
        for which in (0, 1):
            repack(g3, gc, which, w * CHUNK, CHUNK)
        down(w)
        if w + 1 < n:
            g_waves[w + 1].last()
        if w + 2 < n:
            g_waves[w + 2].onward()
        if w + 4 < n:
            g_waves[w + 4].spread()

    for which in (0, 1):
        at = pl.ds(which * half, half)
        act_grad = lax.dot_general(
            gc[at, :], wd[...], (((1,), (1,)), ((), ())), preferred_element_type=F32
        )
        g_val, u_val = gate[at, :], up[at, :]
        sig = jax.nn.sigmoid(g_val)
        gb[at, :] = (act_grad * u_val * sig * (1.0 + g_val * (1.0 - sig))).astype(BF16)
        ub[at, :] = (act_grad * (g_val * sig)).astype(BF16)
    loads[4].wait()
    loads[5].wait()
    for piece in range(pieces):
        at = pl.ds(piece * CHUNK, CHUNK)
        turned = xc[:, at].T
        mg[at, :] = advance(
            wg[at, :], mg[at, :], jnp.dot(turned, gb[...], preferred_element_type=F32)
        )
        gossip(1, piece).start()
        mu[at, :] = advance(
            wu[at, :], mu[at, :], jnp.dot(turned, ub[...], preferred_element_type=F32)
        )
        gossip(2, piece).start()

    for copy in sent:
        copy.wait_send()

    def partial(kind, which, at):
        part = pl.ds(which * half, half)
        if kind == 0:
            return jnp.dot(act[part, :], wd[:, at], preferred_element_type=F32)
        nt = (((1,), (1,)), ((), ()))
        return lax.dot_general(
            gb[part, :], wg[at, :], nt, preferred_element_type=F32
        ) + lax.dot_general(ub[part, :], wu[at, :], nt, preferred_element_type=F32)

    def pair_copy(kind, piece):
        stage, theirs = ((x3, sx), (g3, sg))[kind]
        at = pl.ds(piece * CHUNK, CHUNK)
        return remote(
            stage.at[pl.ds((1 - core) * blocks, blocks), :, at],
            theirs.at[:, :, at],
            pair_send.at[kind, piece],
            pair_recv.at[kind, piece],
            sibling,
        )

    def sum_copy(kind, k):
        stage, theirs = ((x3, px), (g3, pg))[kind]
        at = core * blocks + turn(s + k // SIDE) * SIDE + turn(f + k % SIDE)
        return remote(
            stage.at[at], theirs.at[k], sum_send.at[kind, k], sum_recv.at[kind, k], peers[k - 1]
        )

    for kind, stage in ((0, x3), (1, g3)):
        for piece in range(pieces):
            at = pl.ds(piece * CHUNK, CHUNK)
            value = partial(kind, 1 - core, at)
            for i in range(blocks):
                stage[(1 - core) * blocks + i, :, at] = value[i * rows : (i + 1) * rows].astype(
                    BF16
                )
            pair_copy(kind, piece).start()
    for kind, stage, theirs in ((0, x3, sx), (1, g3, sg)):
        for piece in range(pieces):
            at = pl.ds(piece * CHUNK, CHUNK)
            value = partial(kind, core, at)
            pair_copy(kind, piece).wait_recv()
            for i in range(blocks):
                stage[core * blocks + i, :, at] = (
                    value[i * rows : (i + 1) * rows] + theirs[i, :, at].astype(F32)
                ).astype(BF16)
        for k in range(1, blocks):
            sum_copy(kind, k).start()

    outs = ((nd_o, rd), (ng_o, rg), (nu_o, ru))
    order = [(0, p) for p in range(pieces)] + [(k, p) for p in range(pieces) for k in (1, 2)]

    def write(kind, piece):
        at = pl.ds(piece * CHUNK, CHUNK)
        index = (slice(None), at) if kind == 0 else (at, slice(None))
        to, theirs = outs[kind]
        return pltpu.make_async_copy(
            theirs.at[index], to.at[(0, *index)], write_sem.at[kind * pieces + piece]
        )

    def finish(kind, piece):
        at = pl.ds(piece * CHUNK, CHUNK)
        index = (slice(None), at) if kind == 0 else (at, slice(None))
        mine, theirs = ((md, rd), (mg, rg), (mu, ru))[kind]
        gossip(kind, piece).wait_recv()
        theirs[index] = ((mine[index].astype(F32) + theirs[index].astype(F32)) * 0.5).astype(BF16)
        write(kind, piece).start()

    for kind, piece in order[:9]:
        finish(kind, piece)
    for kind, given, stage, theirs, to in (
        (0, x_in, x3, px, out_o),
        (1, g_in, g3, pg, gin_o),
    ):
        for k in range(1, blocks):
            sum_copy(kind, k).wait_recv()
        mine = core * blocks + s * SIDE + f
        for piece in range(pieces):
            at = pl.ds(piece * CHUNK, CHUNK)
            total = stage[mine, :, at].astype(F32)
            for k in range(1, blocks):
                total = total + theirs[k, :, at].astype(F32)
            to[:, at] = total
    for kind, piece in order[9:]:
        finish(kind, piece)
    for kind in (0, 1):
        for piece in range(pieces):
            pair_copy(kind, piece).wait_send()
        for k in range(1, blocks):
            sum_copy(kind, k).wait_send()
    for kind, piece in order:
        gossip(kind, piece).wait_send()
        write(kind, piece).wait()


def call(level, *args):
    x_in, _, wg, _, wd = args[:5]
    rows, depth = x_in.shape
    width = wg.shape[2]
    blocks = SIDE * SIDE
    tokens = 2 * blocks * rows
    pieces = depth // CHUNK
    any_space = pl.BlockSpec(memory_space=pl.ANY)
    vmem = pl.BlockSpec(memory_space=pltpu.VMEM)
    dma = pltpu.SemaphoreType.DMA
    tall, flat = pltpu.VMEM((depth, width), BF16), pltpu.VMEM((width, depth), BF16)
    return pl.pallas_call(
        functools.partial(kernel, level),
        name="step_level_" + str(level),
        out_shape=(
            jax.ShapeDtypeStruct((rows, depth), F32),
            jax.ShapeDtypeStruct((rows, depth), F32),
            jax.ShapeDtypeStruct(wg.shape, BF16),
            jax.ShapeDtypeStruct(wg.shape, BF16),
            jax.ShapeDtypeStruct(wd.shape, BF16),
        ),
        in_specs=[any_space] * 8,
        out_specs=(vmem, vmem, any_space, any_space, any_space),
        scratch_shapes=[
            pltpu.VMEM((2 * blocks, rows, depth), BF16),
            pltpu.VMEM((2 * blocks, rows, depth), BF16),
            pltpu.VMEM((tokens, depth), BF16),
            pltpu.VMEM((tokens, depth), BF16),
            tall,
            tall,
            flat,
            tall,
            tall,
            flat,
            tall,
            tall,
            flat,
            pltpu.VMEM((tokens, width), F32),
            pltpu.VMEM((tokens, width), F32),
            pltpu.VMEM((tokens, width), BF16),
            pltpu.VMEM((tokens, width), BF16),
            pltpu.VMEM((tokens, width), BF16),
            pltpu.VMEM((width, tokens), BF16),
            pltpu.VMEM((blocks, rows, depth), BF16),
            pltpu.VMEM((blocks, rows, depth), BF16),
            pltpu.VMEM((blocks, rows, depth), BF16),
            pltpu.VMEM((blocks, rows, depth), BF16),
            dma((6,)),
            dma((1 + pieces,)),
            dma((1 + pieces, 24)),
            dma((1 + pieces, 24)),
            dma((2, pieces)),
            dma((2, pieces)),
            dma((2, blocks)),
            dma((2, blocks)),
            dma((3 * pieces,)),
            dma((3 * pieces,)),
            dma((3 * pieces,)),
        ],
        compiler_params=pltpu.CompilerParams(
            collective_id=level, has_side_effects=True, vmem_limit_bytes=60 << 20
        ),
    )(*args)


def per_device(*args):
    *arrays, step_count = args
    levels = (lax.axis_size("rep") // SPLIT).bit_length() - 1
    out, back, *weights = lax.switch(
        jnp.mod(step_count, levels),
        [functools.partial(call, level) for level in range(levels)],
        *arrays,
    )
    block_out = (arrays[0].astype(F32) + out).astype(BF16)
    input_grad = (arrays[1].astype(F32) + back).astype(BF16)
    return (block_out, input_grad, *weights)


def solution(mesh):
    rows, columns, across = P(("rep", "tp"), None), P("rep", None, "tp"), P("rep", "tp", None)
    return jax.shard_map(
        per_device,
        mesh=mesh,
        in_specs=(rows, rows, columns, columns, across, columns, columns, across, P()),
        out_specs=(rows, rows, columns, columns, across),
        check_vma=False,
    )
```

```python
import functools

import jax
import jax.numpy as jnp
from jax import lax
from jax.experimental import pallas as pl
from jax.experimental.pallas import tpu as pltpu
from jax.sharding import PartitionSpec as P

MESH = pl.DeviceIdType.MESH
SPLIT = 4
SIDE = 4
MOMENT = 0.9
LEARN = 0.001
CHUNK = 512
FLAGS = ()
EARLY = (192, 80, 80)
F32 = jnp.float32
BF16 = jnp.bfloat16


def at_multiple(index, of):
    return pl.multiple_of(index, of)


def kernel(
    level,
    x_in,
    g_in,
    wg_in,
    wu_in,
    wd_in,
    mg_in,
    mu_in,
    md_in,
    out_o,
    gin_o,
    ng_o,
    nu_o,
    nd_o,
    x3,
    g3,
    xc,
    gc,
    wg,
    wu,
    wd,
    mg,
    mu,
    md,
    rg,
    ru,
    rd,
    gate,
    up,
    act,
    gb,
    ub,
    actt,
    he,
    gp3,
    actp,
    sx,
    sg,
    px,
    pg,
    load_sem,
    own_sem,
    wave_send,
    wave_recv,
    pair_send,
    pair_recv,
    sum_send,
    sum_recv,
    gossip_send,
    gossip_recv,
    write_sem,
):
    rows, depth = x_in.shape
    width = wg.shape[1]
    blocks = SIDE * SIDE
    half = blocks * rows
    r, t = lax.axis_index("rep"), lax.axis_index("tp")
    z, core = r // SPLIT, r % 2
    x, y = (r // 2) % 2 * 2 + t // SIDE, t % SIDE
    s = x + core * (y - x)
    f = y + core * (x - y)

    def turn(index):
        return (index + SIDE) % SIDE

    def device(cc, ss, ff, zz=None):
        xx = ss + cc * (ff - ss)
        yy = ff + cc * (ss - ff)
        return ((z if zz is None else zz) * SPLIT + xx // 2 * 2 + cc, xx % 2 * SIDE + yy)

    f_plus, f_minus = device(core, s, turn(f + 1)), device(core, s, turn(f - 1))
    s_plus, s_minus = device(core, turn(s + 1), f), device(core, turn(s - 1), f)
    sibling = (z * SPLIT + x // 2 * 2 + 1 - core, t)
    step = 2**level
    partner_z = z + step - 2 * step * (z // step % 2)
    partner = device(core, s, f, partner_z)
    s_peers = [device(core, turn(s + k), f) for k in range(1, SIDE)]
    f_peers = [device(core, s, turn(f + k)) for k in range(1, SIDE)]

    def remote(src, dst, send, recv, to):
        return pltpu.make_async_remote_copy(
            src_ref=src, dst_ref=dst, send_sem=send, recv_sem=recv, device_id=to, device_id_type=MESH
        )

    loads = [
        pltpu.make_async_copy(src.at[0], dst, load_sem.at[i])
        for i, (src, dst) in enumerate(
            ((wd_in, wd), (md_in, md), (wg_in, wg), (wu_in, wu), (mg_in, mg), (mu_in, mu))
        )
    ]
    pieces = depth // CHUNK

    def when(condition, run):
        if isinstance(condition, bool):
            if condition:
                run()
        else:
            pl.when(condition)(run)

    class Wave:
        def __init__(self, w, src, land, col, wide):
            self.w, self.src, self.land, self.col, self.wide = w, src, land, col, wide

        def cols(self, part):
            wide = self.wide
            if part == "all":
                return pl.ds(self.col, wide)
            return pl.ds(self.col + (wide // 2 if part == "high" else 0), wide // 2)

        def block(self, ds, df, part="all"):
            at = core * blocks + turn(s + ds) * SIDE + turn(f + df)
            return self.land.at[at, :, self.cols(part)]

        def group(self, ds, part="all", other=False):
            if other:
                at = (1 - core) * blocks + turn(f + ds) * SIDE
            else:
                at = core * blocks + turn(s + ds) * SIDE
            return self.land.at[pl.ds(at, SIDE), :, self.cols(part)]

        def copy(self, src, dst, slot, to):
            return remote(src, dst, wave_send.at[self.w, slot], wave_recv.at[self.w, slot], to)

        def send(self, src, dst, slot, to):
            self.copy(src, dst, slot, to).start()

        def wait(self, dst, slot):
            self.copy(dst, dst, slot, sibling).wait_recv()

        def own(self):
            return pltpu.make_async_copy(
                self.src.at[:, self.cols("all")], self.block(0, 0), own_sem.at[self.w]
            )

        def start(self):
            to = self.block(0, 0)
            mine = to if self.src is None else self.src.at[:, self.cols("all")]
            self.send(mine, to, 0, f_plus)
            self.send(mine, to, 1, f_minus)
            if self.src is not None:
                self.own().start()

        def near(self):
            self.wait(self.block(0, -1), 0)
            self.wait(self.block(0, 1), 1)
            for df, part, slot, to in ((-1, "low", 2, f_plus), (1, "high", 3, f_minus)):
                ref = self.block(0, df, part)
                self.send(ref, ref, slot, to)

        def far(self):
            self.wait(self.block(0, 2, "low"), 2)
            self.wait(self.block(0, 2, "high"), 3)

        def to_sibling(self, ds, slot):
            ref = self.group(ds)
            self.send(ref, ref, 20 + slot, sibling)

        def spread(self):
            self.far()
            if self.src is not None:
                self.own().wait()
            ref = self.group(0)
            self.send(ref, ref, 4, s_plus)
            self.send(ref, ref, 8, s_minus)
            self.to_sibling(0, 0)

        def onward(self):
            for ds, part, slot, to in ((-1, "low", 4, s_plus), (1, "high", 8, s_minus)):
                self.wait(self.group(ds), slot)
                ref = self.group(ds, part)
                self.send(ref, ref, slot + 8, to)
            self.to_sibling(-1, 1)
            self.to_sibling(1, 2)

        def last(self):
            self.wait(self.group(2, "low"), 12)
            self.wait(self.group(2, "high"), 16)
            self.to_sibling(2, 3)

        def other(self):
            for slot, ds in enumerate((0, -1, 1, 2)):
                self.wait(self.group(ds, other=True), 20 + slot)

        def sent(self):
            for slot in (0, 1):
                self.copy(self.block(0, 0), self.block(0, 0), slot, sibling).wait_send()
            for slot, part in ((2, "low"), (3, "high")):
                self.copy(self.block(0, 0, part), self.block(0, 0, part), slot, sibling).wait_send()
            for slot in (20, 21, 22, 23):
                self.copy(self.group(0), self.group(0), slot, sibling).wait_send()

        def sent_groups(self):
            for slot, part in ((4, "all"), (8, "all"), (12, "low"), (16, "high")):
                self.copy(self.group(0, part), self.group(0, part), slot, sibling).wait_send()

        def spread_block(self, df, src=None):
            ref = self.block(0, df)
            src = ref if src is None else src
            self.send(src, ref, 4 + df % SIDE, s_plus)
            self.send(src, ref, 8 + df % SIDE, s_minus)

        def onward_block(self, df):
            for ds, part, slot, to in ((-1, "low", 4, s_plus), (1, "high", 8, s_minus)):
                self.wait(self.block(ds, df), slot + df % SIDE)
                ref = self.block(ds, df, part)
                self.send(ref, ref, slot + 8 + df % SIDE, to)

        def last_block(self, df):
            self.wait(self.block(2, df, "low"), 12 + df % SIDE)
            self.wait(self.block(2, df, "high"), 16 + df % SIDE)

        def sent_blocks(self):
            for slot, part in ((4, "all"), (8, "all"), (12, "low"), (16, "high")):
                for df in range(SIDE):
                    ref = self.block(0, 0, part)
                    self.copy(ref, ref, slot + df, sibling).wait_send()

    first = Wave(0, x_in, x3, 0, depth)
    peer_g = Wave(1 + pieces, None, gp3, 0, depth)

    def g_wave(i):
        col = i * CHUNK if isinstance(i, int) else at_multiple(i * CHUNK, CHUNK)
        return Wave(1 + i, g_in, g3, col, CHUNK)

    def piece_at(piece):
        return pl.ds(
            piece * CHUNK if isinstance(piece, int) else at_multiple(piece * CHUNK, CHUNK), CHUNK
        )

    def repack(land, flat, start, pairs, cols):
        def body(i, carry):
            b = start + 2 * i
            pair = jnp.concatenate(
                [land[b, :, cols].astype(F32), land[b + 1, :, cols].astype(F32)], 0
            )
            flat[pl.ds(at_multiple(b * rows, 2 * rows), 2 * rows), cols] = pair.astype(BF16)
            return carry

        lax.fori_loop(0, pairs, body, 0)

    def forward(which):
        at = pl.ds(at_multiple(which * half, half), half)
        tokens = xc[at, :]
        g_val = jnp.dot(tokens, wg[...], preferred_element_type=F32)
        gate[at, :] = g_val
        u_val = jnp.dot(tokens, wu[...], preferred_element_type=F32)
        up[at, :] = u_val
        act[at, :] = (g_val * jax.nn.sigmoid(g_val) * u_val).astype(BF16)

    def advance(weight, moment, grad):
        total = MOMENT * moment.astype(F32) + grad
        return (weight.astype(F32) - LEARN * total).astype(BF16)

    weights = ((md, rd, nd_o), (mg, rg, ng_o), (mu, ru, nu_o), (md, rd, nd_o))
    early = EARLY[level]
    rows_early = pl.ds(0, early)
    mine_at = core * blocks + s * SIDE + f
    ahead = [
        remote(src, dst, gossip_send.at[3 * pieces + i], gossip_recv.at[3 * pieces + i], partner)
        for i, (src, dst) in enumerate(
            (
                (g_in, gp3.at[mine_at]),
                (he.at[rows_early], rd.at[rows_early]),
                (actt.at[rows_early], actp.at[rows_early]),
            )
        )
    ]

    def index_of(kind, at):
        if kind == 0:
            return (pl.ds(early, width - early), at)
        return (at, slice(None)) if kind < 3 else (pl.ds(0, early), at)

    def gossip(kind, piece):
        mine, theirs, _ = weights[kind]
        index = index_of(kind, piece_at(piece))
        n = kind * pieces + piece
        return remote(
            mine.at[index], theirs.at[index], gossip_send.at[n], gossip_recv.at[n], partner
        )

    def gossip_start(kind, piece):
        gossip(kind, piece).start()

    def write(kind, piece):
        index = index_of(kind, piece_at(piece))
        _, theirs, to = weights[kind]
        return pltpu.make_async_copy(
            theirs.at[index], to.at[(0, *index)], write_sem.at[kind * pieces + piece]
        )

    def finish(kind, piece):
        index = index_of(kind, piece_at(piece))
        mine, theirs, _ = weights[kind]
        gossip(kind, piece).wait_recv()
        theirs[index] = ((mine[index].astype(F32) + theirs[index].astype(F32)) * 0.5).astype(BF16)
        write(kind, piece).start()

    def repeat(count, run, start=0):
        def body(i, carry):
            run(i)
            return carry

        lax.fori_loop(start, count, body, 0)

    compute = "nocompute" not in FLAGS

    for load in loads:
        load.start()
    barrier = pltpu.get_barrier_semaphore()
    greeted = s_peers + f_peers + [sibling, partner]
    for to in greeted:
        pl.semaphore_signal(barrier, inc=1, device_id=to, device_id_type=MESH)
    pl.semaphore_wait(barrier, len(greeted))

    first.start()
    first.spread_block(0, x_in.at[:, pl.ds(0, depth)])
    ahead[0].start()
    loads[0].wait()
    loads[1].wait()

    def decayed(piece):
        at = piece_at(piece)
        he[rows_early, at] = advance(wd[rows_early, at], md[rows_early, at], 0.0)

    repeat(pieces, decayed)
    ahead[1].start()
    first.near()
    first.spread_block(-1)
    first.spread_block(1)
    first.onward_block(0)
    first.far()
    first.spread_block(2)
    first.own().wait()
    first.to_sibling(0, 0)
    first.onward_block(-1)
    first.onward_block(1)
    repeat(pieces, lambda i: g_wave(i).start())
    first.onward_block(2)
    first.to_sibling(-1, 1)
    first.to_sibling(1, 2)
    repeat(pieces, lambda i: g_wave(i).near())
    repeat(2, lambda i: g_wave(i).spread())

    def token_half(i):
        def own_half():
            for df in (0, -1, 1, 2):
                first.last_block(df)
            first.to_sibling(2, 3)
            loads[2].wait()
            loads[3].wait()
            g_wave(0).onward()

        def other_half():
            first.other()
            g_wave(0).last()
            g_wave(1).onward()

        when(i == 0, own_half)
        when(i == 1, other_half)
        which = core + i * (1 - 2 * core)
        if compute:
            repack(x3, xc, which * blocks, blocks // 2, pl.ds(0, depth))
            forward(which)
        when(i == 0, lambda: g_wave(2).spread())
        when(i == 1, lambda: g_wave(3).spread())

    repeat(2, token_half)
    if compute:
        actt[...] = act[...].T
    ahead[2].start()

    def down(w):
        g_wave(w).other()
        at = piece_at(w)
        if compute:
            repack(g3, gc, 0, blocks, at)
            grad = jnp.dot(actt[...], gc[:, at], preferred_element_type=F32)
            md[:, at] = advance(wd[:, at], md[:, at], grad)
        gossip_start(0, w)
        when(w + 1 < pieces, lambda: g_wave(w + 1).last())
        when(w + 2 < pieces, lambda: g_wave(w + 2).onward())
        when(w + 4 < pieces, lambda: g_wave(w + 4).spread())

    repeat(pieces, down)

    def backward(which):
        at = pl.ds(at_multiple(which * half, half), half)
        act_grad = lax.dot_general(
            gc[at, :], wd[...], (((1,), (1,)), ((), ())), preferred_element_type=F32
        )
        g_val, u_val = gate[at, :], up[at, :]
        sig = jax.nn.sigmoid(g_val)
        gb[at, :] = (act_grad * u_val * sig * (1.0 + g_val * (1.0 - sig))).astype(BF16)
        ub[at, :] = (act_grad * (g_val * sig)).astype(BF16)

    ahead[0].wait_recv()
    peer_g.start()
    if compute:
        repeat(2, backward)
    peer_g.near()
    loads[4].wait()
    loads[5].wait()

    def columns(piece):
        at = piece_at(piece)
        if compute:
            turned = xc[:, at].T
            mg[at, :] = advance(
                wg[at, :], mg[at, :], jnp.dot(turned, gb[...], preferred_element_type=F32)
            )
        gossip_start(1, piece)
        if compute:
            mu[at, :] = advance(
                wu[at, :], mu[at, :], jnp.dot(turned, ub[...], preferred_element_type=F32)
            )
        gossip_start(2, piece)

    repeat(pieces, columns)

    first.sent()
    first.sent_blocks()

    def g_sent(i):
        g_wave(i).sent()
        g_wave(i).sent_groups()

    repeat(pieces, g_sent)

    def partial(kind, which, at):
        part = pl.ds(at_multiple(which * half, half), half)
        if kind == 0:
            return jnp.dot(act[part, :], wd[:, at], preferred_element_type=F32)
        nt = (((1,), (1,)), ((), ()))
        return lax.dot_general(
            gb[part, :], wg[at, :], nt, preferred_element_type=F32
        ) + lax.dot_general(ub[part, :], wu[at, :], nt, preferred_element_type=F32)

    sums = ((x3, sx, px, out_o), (g3, sg, pg, gin_o))

    def pair_copy(kind, piece):
        stage, theirs, _, _ = sums[kind]
        at = piece_at(piece)
        return remote(
            stage.at[pl.ds((1 - core) * blocks, blocks), :, at],
            theirs.at[:, :, at],
            pair_send.at[kind, piece],
            pair_recv.at[kind, piece],
            sibling,
        )

    def s_copy(kind, k):
        stage, _, theirs, _ = sums[kind]
        return remote(
            stage.at[pl.ds(core * blocks + turn(s + k) * SIDE, SIDE)],
            theirs.at[pl.ds(k * SIDE, SIDE)],
            sum_send.at[kind, k],
            sum_recv.at[kind, k],
            s_peers[k - 1],
        )

    def f_copy(kind, k):
        stage, _, theirs, _ = sums[kind]
        return remote(
            stage.at[core * blocks + s * SIDE + turn(f + k)],
            theirs.at[k],
            sum_send.at[kind, SIDE + k],
            sum_recv.at[kind, SIDE + k],
            f_peers[k - 1],
        )

    def for_sibling(kind, piece):
        stage = sums[kind][0]
        at = piece_at(piece)
        value = partial(kind, 1 - core, at)
        for i in range(blocks):
            stage[(1 - core) * blocks + i, :, at] = value[i * rows : (i + 1) * rows].astype(BF16)
        pair_copy(kind, piece).start()

    def with_sibling(kind, piece):
        stage, theirs, _, _ = sums[kind]
        at = piece_at(piece)
        value = partial(kind, core, at)
        pair_copy(kind, piece).wait_recv()
        for i in range(blocks):
            stage[core * blocks + i, :, at] = (
                value[i * rows : (i + 1) * rows] + theirs[i, :, at].astype(F32)
            ).astype(BF16)

    def along_s(kind):
        stage, _, theirs, _ = sums[kind]
        for k in range(1, SIDE):
            s_copy(kind, k).wait_recv()

        def add(i):
            b = core * blocks + s * SIDE + i
            value = stage[b].astype(F32)
            for k in range(1, SIDE):
                value = value + theirs[k * SIDE + i].astype(F32)
            stage[b] = value.astype(BF16)

        repeat(SIDE, add)
        for k in range(1, SIDE):
            f_copy(kind, k).start()

    def total(kind):
        stage, _, theirs, to = sums[kind]
        for k in range(1, SIDE):
            f_copy(kind, k).wait_recv()
        value = stage[mine_at].astype(F32)
        for k in range(1, SIDE):
            value = value + theirs[k].astype(F32)
        to[...] = value

    peer_g.spread()
    repeat(pieces, functools.partial(for_sibling, 0))
    peer_g.onward()
    repeat(pieces, functools.partial(for_sibling, 1))
    peer_g.last()
    for kind in (0, 1):
        repeat(pieces, functools.partial(with_sibling, kind))
        for k in range(1, SIDE):
            s_copy(kind, k).start()

    peer_g.other()
    repack(gp3, gc, 0, blocks, pl.ds(0, depth))
    ahead[1].wait_recv()
    ahead[2].wait_recv()

    def peer_rows(piece):
        at = piece_at(piece)
        grad = jnp.dot(actp[rows_early, :], gc[:, at], preferred_element_type=F32)
        theirs = (rd[rows_early, at].astype(F32) - LEARN * grad).astype(BF16)
        both = md[rows_early, at].astype(F32) + theirs.astype(F32)
        rd[rows_early, at] = (both * 0.5).astype(BF16)
        write(3, piece).start()

    repeat(pieces, peer_rows)
    for kind in (0, 1):
        along_s(kind)

    repeat(pieces, functools.partial(finish, 0))

    def finish_both(piece):
        finish(1, piece)
        finish(2, piece)

    repeat(pieces - 3, finish_both)
    for kind in (0, 1):
        total(kind)
    repeat(pieces, finish_both, pieces - 3)

    peer_g.sent()
    peer_g.sent_groups()
    for kind in (0, 1):
        repeat(pieces, lambda piece: pair_copy(kind, piece).wait_send())
        for k in range(1, SIDE):
            s_copy(kind, k).wait_send()
            f_copy(kind, k).wait_send()
    for copy in ahead:
        copy.wait_send()
    for kind in range(4):
        if kind < 3:
            repeat(pieces, lambda piece: gossip(kind, piece).wait_send())
        repeat(pieces, lambda piece: write(kind, piece).wait())


def call(level, *args):
    x_in, _, wg, _, wd = args[:5]
    rows, depth = x_in.shape
    width = wg.shape[2]
    blocks = SIDE * SIDE
    tokens = 2 * blocks * rows
    pieces = depth // CHUNK
    any_space = pl.BlockSpec(memory_space=pl.ANY)
    vmem = pl.BlockSpec(memory_space=pltpu.VMEM)
    dma = pltpu.SemaphoreType.DMA
    tall, flat = pltpu.VMEM((depth, width), BF16), pltpu.VMEM((width, depth), BF16)
    return pl.pallas_call(
        functools.partial(kernel, level),
        name="step_level_" + str(level),
        out_shape=(
            jax.ShapeDtypeStruct((rows, depth), F32),
            jax.ShapeDtypeStruct((rows, depth), F32),
            jax.ShapeDtypeStruct(wg.shape, BF16),
            jax.ShapeDtypeStruct(wg.shape, BF16),
            jax.ShapeDtypeStruct(wd.shape, BF16),
        ),
        in_specs=[any_space] * 8,
        out_specs=(vmem, vmem, any_space, any_space, any_space),
        scratch_shapes=[
            pltpu.VMEM((2 * blocks, rows, depth), BF16),
            pltpu.VMEM((2 * blocks, rows, depth), BF16),
            pltpu.VMEM((tokens, depth), BF16),
            pltpu.VMEM((tokens, depth), BF16),
            tall,
            tall,
            flat,
            tall,
            tall,
            flat,
            tall,
            tall,
            flat,
            pltpu.VMEM((tokens, width), F32),
            pltpu.VMEM((tokens, width), F32),
            pltpu.VMEM((tokens, width), BF16),
            pltpu.VMEM((tokens, width), BF16),
            pltpu.VMEM((tokens, width), BF16),
            pltpu.VMEM((width, tokens), BF16),
            pltpu.VMEM((max(EARLY), depth), BF16),
            pltpu.VMEM((2 * blocks, rows, depth), BF16),
            pltpu.VMEM((max(EARLY), tokens), BF16),
            pltpu.VMEM((blocks, rows, depth), BF16),
            pltpu.VMEM((blocks, rows, depth), BF16),
            pltpu.VMEM((blocks, rows, depth), BF16),
            pltpu.VMEM((blocks, rows, depth), BF16),
            dma((6,)),
            dma((1 + pieces,)),
            dma((2 + pieces, 24)),
            dma((2 + pieces, 24)),
            dma((2, pieces)),
            dma((2, pieces)),
            dma((2, 2 * SIDE)),
            dma((2, 2 * SIDE)),
            dma((3 * pieces + 3,)),
            dma((3 * pieces + 3,)),
            dma((4 * pieces,)),
        ],
        compiler_params=pltpu.CompilerParams(
            collective_id=level, has_side_effects=True, vmem_limit_bytes=60 << 20
        ),
    )(*args)


def per_device(*args):
    *arrays, step_count = args
    levels = (lax.axis_size("rep") // SPLIT).bit_length() - 1
    out, back, *weights = lax.switch(
        jnp.mod(step_count, levels),
        [functools.partial(call, level) for level in range(levels)],
        *arrays,
    )
    block_out = (arrays[0].astype(F32) + out).astype(BF16)
    input_grad = (arrays[1].astype(F32) + back).astype(BF16)
    return (block_out, input_grad, *weights)


def solution(mesh):
    rows, columns, across = P(("rep", "tp"), None), P("rep", None, "tp"), P("rep", "tp", None)
    return jax.shard_map(
        per_device,
        mesh=mesh,
        in_specs=(rows, rows, columns, columns, across, columns, columns, across, P()),
        out_specs=(rows, rows, columns, columns, across),
        check_vma=False,
    )
```

```python
import functools

import jax
import jax.numpy as jnp
from jax import lax
from jax.experimental import pallas as pl
from jax.experimental.pallas import tpu as pltpu
from jax.sharding import PartitionSpec as P

MESH = pl.DeviceIdType.MESH
SPLIT = 4
SIDE = 4
MOMENT = 0.9
LEARN = 0.001
CHUNK = 512
EARLY = (192, 96, 96)
F32 = jnp.float32
BF16 = jnp.bfloat16


def at_multiple(index, of):
    return pl.multiple_of(index, of)


def kernel(
    level,
    x_in,
    g_in,
    wg_in,
    wu_in,
    wd_in,
    mg_in,
    mu_in,
    md_in,
    out_o,
    gin_o,
    ng_o,
    nu_o,
    nd_o,
    x3,
    g3,
    xc,
    gc,
    wg,
    wu,
    wd,
    mg,
    mu,
    md,
    rg,
    ru,
    rd,
    gate,
    up,
    act,
    gb,
    ub,
    actt,
    he,
    gp3,
    actp,
    sx,
    sg,
    px,
    pg,
    xo,
    go,
    load_sem,
    own_sem,
    wave_send,
    wave_recv,
    pair_send,
    pair_recv,
    sum_send,
    sum_recv,
    gossip_send,
    gossip_recv,
):
    rows, depth = x_in.shape
    width = wg.shape[1]
    blocks = SIDE * SIDE
    half = blocks * rows
    r, t = lax.axis_index("rep"), lax.axis_index("tp")
    z, core = r // SPLIT, r % 2
    x, y = (r // 2) % 2 * 2 + t // SIDE, t % SIDE
    s = x + core * (y - x)
    f = y + core * (x - y)

    def turn(index):
        return (index + SIDE) % SIDE

    def device(cc, ss, ff, zz=None):
        xx = ss + cc * (ff - ss)
        yy = ff + cc * (ss - ff)
        return ((z if zz is None else zz) * SPLIT + xx // 2 * 2 + cc, xx % 2 * SIDE + yy)

    f_plus, f_minus = device(core, s, turn(f + 1)), device(core, s, turn(f - 1))
    s_plus, s_minus = device(core, turn(s + 1), f), device(core, turn(s - 1), f)
    sibling = (z * SPLIT + x // 2 * 2 + 1 - core, t)
    step = 2**level
    partner_z = z + step - 2 * step * (z // step % 2)
    partner = device(core, s, f, partner_z)
    s_peers = [device(core, turn(s + k), f) for k in range(1, SIDE)]
    f_peers = [device(core, s, turn(f + k)) for k in range(1, SIDE)]

    def remote(src, dst, send, recv, to):
        return pltpu.make_async_remote_copy(
            src_ref=src, dst_ref=dst, send_sem=send, recv_sem=recv, device_id=to, device_id_type=MESH
        )

    loads = [
        pltpu.make_async_copy(src.at[0], dst, load_sem.at[i])
        for i, (src, dst) in enumerate(
            ((wd_in, wd), (md_in, md), (wg_in, wg), (wu_in, wu), (mg_in, mg), (mu_in, mu))
        )
    ]
    loads += [
        pltpu.make_async_copy(src, dst, load_sem.at[6 + i])
        for i, (src, dst) in enumerate(((x_in, xo), (g_in, go)))
    ]
    pieces = depth // CHUNK

    def when(condition, run):
        if isinstance(condition, bool):
            if condition:
                run()
        else:
            pl.when(condition)(run)

    class Wave:
        def __init__(self, w, src, land, col, wide):
            self.w, self.src, self.land, self.col, self.wide = w, src, land, col, wide

        def cols(self, part):
            wide = self.wide
            if part == "all":
                return pl.ds(self.col, wide)
            return pl.ds(self.col + (wide // 2 if part == "high" else 0), wide // 2)

        def block(self, ds, df, part="all"):
            at = core * blocks + turn(s + ds) * SIDE + turn(f + df)
            return self.land.at[at, :, self.cols(part)]

        def group(self, ds, part="all", other=False):
            if other:
                at = (1 - core) * blocks + turn(f + ds) * SIDE
            else:
                at = core * blocks + turn(s + ds) * SIDE
            return self.land.at[pl.ds(at, SIDE), :, self.cols(part)]

        def copy(self, src, dst, slot, to):
            return remote(src, dst, wave_send.at[self.w, slot], wave_recv.at[self.w, slot], to)

        def send(self, src, dst, slot, to):
            self.copy(src, dst, slot, to).start()

        def wait(self, dst, slot):
            self.copy(dst, dst, slot, sibling).wait_recv()

        def own(self):
            return pltpu.make_async_copy(
                self.src.at[:, self.cols("all")], self.block(0, 0), own_sem.at[self.w]
            )

        def start(self):
            to = self.block(0, 0)
            mine = to if self.src is None else self.src.at[:, self.cols("all")]
            self.send(mine, to, 0, f_plus)
            self.send(mine, to, 1, f_minus)
            if self.src is not None:
                self.own().start()

        def near(self):
            self.wait(self.block(0, -1), 0)
            self.wait(self.block(0, 1), 1)
            for df, part, slot, to in ((-1, "low", 2, f_plus), (1, "high", 3, f_minus)):
                ref = self.block(0, df, part)
                self.send(ref, ref, slot, to)

        def far(self):
            self.wait(self.block(0, 2, "low"), 2)
            self.wait(self.block(0, 2, "high"), 3)

        def to_sibling(self, ds, slot):
            ref = self.group(ds)
            self.send(ref, ref, 20 + slot, sibling)

        def spread(self):
            self.far()
            if self.src is not None:
                self.own().wait()
            ref = self.group(0)
            self.send(ref, ref, 4, s_plus)
            self.send(ref, ref, 8, s_minus)
            self.to_sibling(0, 0)

        def onward(self):
            for ds, part, slot, to in ((-1, "low", 4, s_plus), (1, "high", 8, s_minus)):
                self.wait(self.group(ds), slot)
                ref = self.group(ds, part)
                self.send(ref, ref, slot + 8, to)
            self.to_sibling(-1, 1)
            self.to_sibling(1, 2)

        def last(self):
            self.wait(self.group(2, "low"), 12)
            self.wait(self.group(2, "high"), 16)
            self.to_sibling(2, 3)

        def other(self):
            for slot, ds in enumerate((0, -1, 1, 2)):
                self.wait(self.group(ds, other=True), 20 + slot)

        def sent(self):
            for slot in (0, 1):
                self.copy(self.block(0, 0), self.block(0, 0), slot, sibling).wait_send()
            for slot, part in ((2, "low"), (3, "high")):
                self.copy(self.block(0, 0, part), self.block(0, 0, part), slot, sibling).wait_send()
            for slot in (20, 21, 22, 23):
                self.copy(self.group(0), self.group(0), slot, sibling).wait_send()

        def sent_groups(self):
            for slot, part in ((4, "all"), (8, "all"), (12, "low"), (16, "high")):
                self.copy(self.group(0, part), self.group(0, part), slot, sibling).wait_send()

        def step(self, n):
            if n == 0:
                self.start()
                self.spread_block(0, self.src.at[:, self.cols("all")])
            elif n == 1:
                self.near()
                self.spread_block(-1)
                self.spread_block(1)
                self.onward_block(0)
            elif n == 2:
                self.far()
                self.spread_block(2)
                self.own().wait()
                self.to_sibling(0, 0)
                self.onward_block(-1)
                self.onward_block(1)
            elif n == 3:
                self.onward_block(2)
                self.to_sibling(-1, 1)
                self.to_sibling(1, 2)
            elif n == 4:
                for df in (0, -1, 1, 2):
                    self.last_block(df)
                self.to_sibling(2, 3)
            else:
                self.other()

        def spread_block(self, df, src=None):
            ref = self.block(0, df)
            src = ref if src is None else src
            self.send(src, ref, 4 + df % SIDE, s_plus)
            self.send(src, ref, 8 + df % SIDE, s_minus)

        def onward_block(self, df):
            for ds, part, slot, to in ((-1, "low", 4, s_plus), (1, "high", 8, s_minus)):
                self.wait(self.block(ds, df), slot + df % SIDE)
                ref = self.block(ds, df, part)
                self.send(ref, ref, slot + 8 + df % SIDE, to)

        def last_block(self, df):
            self.wait(self.block(2, df, "low"), 12 + df % SIDE)
            self.wait(self.block(2, df, "high"), 16 + df % SIDE)

        def sent_blocks(self):
            for slot, part in ((4, "all"), (8, "all"), (12, "low"), (16, "high")):
                for df in range(SIDE):
                    ref = self.block(0, 0, part)
                    self.copy(ref, ref, slot + df, sibling).wait_send()

    first = Wave(0, x_in, x3, 0, depth)
    g_waves = [Wave(1 + i, g_in, g3, i * depth // 2, depth // 2) for i in (0, 1)]
    peer_g = Wave(3, None, gp3, 0, depth)

    def piece_at(piece):
        return pl.ds(
            piece * CHUNK if isinstance(piece, int) else at_multiple(piece * CHUNK, CHUNK), CHUNK
        )

    def repack(land, flat, start, pairs, cols):
        def body(i, carry):
            b = start + 2 * i
            pair = jnp.concatenate(
                [land[b, :, cols].astype(F32), land[b + 1, :, cols].astype(F32)], 0
            )
            flat[pl.ds(at_multiple(b * rows, 2 * rows), 2 * rows), cols] = pair.astype(BF16)
            return carry

        lax.fori_loop(0, pairs, body, 0)

    def forward(which):
        at = pl.ds(at_multiple(which * half, half), half)
        tokens = xc[at, :]
        g_val = jnp.dot(tokens, wg[...], preferred_element_type=F32)
        gate[at, :] = g_val
        u_val = jnp.dot(tokens, wu[...], preferred_element_type=F32)
        up[at, :] = u_val
        act[at, :] = (g_val * jax.nn.sigmoid(g_val) * u_val).astype(BF16)

    def advance(weight, moment, grad):
        total = MOMENT * moment.astype(F32) + grad
        return (weight.astype(F32) - LEARN * total).astype(BF16)

    weights = ((md, rd, nd_o), (mg, rg, ng_o), (mu, ru, nu_o))
    early = EARLY[level]
    rows_early = pl.ds(0, early)
    mine_at = core * blocks + s * SIDE + f
    ahead = [
        remote(src, dst, gossip_send.at[3 * pieces + i], gossip_recv.at[3 * pieces + i], partner)
        for i, (src, dst) in enumerate(
            (
                (g_in, gp3.at[mine_at]),
                (he.at[rows_early], rd.at[rows_early]),
                (actt.at[rows_early], actp.at[rows_early]),
            )
        )
    ]

    def index_of(kind, at):
        if kind == 0:
            return (pl.ds(early, width - early), at)
        return (at, slice(None))

    def gossip(kind, piece):
        mine, theirs, _ = weights[kind]
        index = index_of(kind, piece_at(piece))
        n = kind * pieces + piece
        return remote(
            mine.at[index], theirs.at[index], gossip_send.at[n], gossip_recv.at[n], partner
        )

    def gossip_start(kind, piece):
        gossip(kind, piece).start()

    def finish(kind, piece):
        index = index_of(kind, piece_at(piece))
        mine, theirs, to = weights[kind]
        gossip(kind, piece).wait_recv()
        both = mine[index].astype(F32) + theirs[index].astype(F32)
        to[(0, *index)] = (both * 0.5).astype(BF16)

    def repeat(count, run, start=0):
        def body(i, carry):
            run(i)
            return carry

        lax.fori_loop(start, count, body, 0)

    def partial(kind, which, at):
        part = pl.ds(at_multiple(which * half, half), half)
        if kind == 0:
            return jnp.dot(act[part, :], wd[:, at], preferred_element_type=F32)
        nt = (((1,), (1,)), ((), ()))
        return lax.dot_general(
            gb[part, :], wg[at, :], nt, preferred_element_type=F32
        ) + lax.dot_general(ub[part, :], wu[at, :], nt, preferred_element_type=F32)

    sums = ((x3, sx, px, out_o), (g3, sg, pg, gin_o))
    given = (xo, go)

    def pair_copy(kind, piece):
        stage, theirs, _, _ = sums[kind]
        at = piece_at(piece)
        return remote(
            stage.at[pl.ds((1 - core) * blocks, blocks), :, at],
            theirs.at[:, :, at],
            pair_send.at[kind, piece],
            pair_recv.at[kind, piece],
            sibling,
        )

    def s_copy(kind, k):
        stage, _, theirs, _ = sums[kind]
        return remote(
            stage.at[pl.ds(core * blocks + turn(s + k) * SIDE, SIDE)],
            theirs.at[pl.ds(k * SIDE, SIDE)],
            sum_send.at[kind, k],
            sum_recv.at[kind, k],
            s_peers[k - 1],
        )

    def f_copy(kind, k):
        stage, _, theirs, _ = sums[kind]
        return remote(
            stage.at[core * blocks + s * SIDE + turn(f + k)],
            theirs.at[k],
            sum_send.at[kind, SIDE + k],
            sum_recv.at[kind, SIDE + k],
            f_peers[k - 1],
        )

    def for_sibling(kind, piece):
        stage = sums[kind][0]
        at = piece_at(piece)
        value = partial(kind, 1 - core, at)
        for i in range(blocks):
            stage[(1 - core) * blocks + i, :, at] = value[i * rows : (i + 1) * rows].astype(BF16)
        pair_copy(kind, piece).start()

    def with_sibling(kind, piece):
        stage, theirs, _, _ = sums[kind]
        at = piece_at(piece)
        value = partial(kind, core, at)
        pair_copy(kind, piece).wait_recv()
        for i in range(blocks):
            stage[core * blocks + i, :, at] = (
                value[i * rows : (i + 1) * rows] + theirs[i, :, at].astype(F32)
            ).astype(BF16)

    def along_s(kind):
        stage, _, theirs, _ = sums[kind]
        for k in range(1, SIDE):
            s_copy(kind, k).wait_recv()

        def add(i):
            b = core * blocks + s * SIDE + i
            value = stage[b].astype(F32)
            for k in range(1, SIDE):
                value = value + theirs[k * SIDE + i].astype(F32)
            stage[b] = value.astype(BF16)

        repeat(SIDE, add)
        for k in range(1, SIDE):
            f_copy(kind, k).start()

    def total(kind):
        stage, _, theirs, to = sums[kind]
        for k in range(1, SIDE):
            f_copy(kind, k).wait_recv()
        value = stage[mine_at].astype(F32)
        for k in range(1, SIDE):
            value = value + theirs[k].astype(F32)
        loads[6 + kind].wait()
        to[...] = (given[kind][...].astype(F32) + value).astype(BF16)

    for load in loads:
        load.start()
    barrier = pltpu.get_barrier_semaphore()
    greeted = s_peers + f_peers + [sibling, partner]
    for to in greeted:
        pl.semaphore_signal(barrier, inc=1, device_id=to, device_id_type=MESH)
    pl.semaphore_wait(barrier, len(greeted))

    first.step(0)
    ahead[0].start()
    loads[0].wait()
    loads[1].wait()

    def decayed(piece):
        at = piece_at(piece)
        he[rows_early, at] = advance(wd[rows_early, at], md[rows_early, at], 0.0)

    repeat(pieces, decayed)
    ahead[1].start()
    first.step(1)
    first.step(2)
    g_waves[0].step(0)
    first.step(3)
    g_waves[0].step(1)
    g_waves[1].step(0)

    def token_half(i):
        def own_half():
            first.step(4)
            loads[2].wait()
            loads[3].wait()

        def other_half():
            g_waves[0].step(2)
            g_waves[1].step(1)
            first.step(5)

        when(i == 0, own_half)
        when(i == 1, other_half)
        which = core + i * (1 - 2 * core)
        repack(x3, xc, which * blocks, blocks // 2, pl.ds(0, depth))
        forward(which)

    repeat(2, token_half)
    g_waves[0].step(3)
    g_waves[1].step(2)
    actt[...] = act[...].T
    ahead[2].start()
    g_waves[0].step(4)
    g_waves[1].step(3)

    def down(piece):
        at = piece_at(piece)
        grad = jnp.dot(actt[...], gc[:, at], preferred_element_type=F32)
        md[:, at] = advance(wd[:, at], md[:, at], grad)
        gossip(0, piece).start()

    g_waves[0].step(5)
    repack(g3, gc, 0, blocks, pl.ds(0, depth // 2))
    repeat(pieces // 2, down)
    first.sent()
    first.sent_blocks()
    g_waves[1].step(4)
    repeat(pieces, functools.partial(for_sibling, 0))
    g_waves[1].step(5)
    repack(g3, gc, 0, blocks, pl.ds(depth // 2, depth // 2))
    repeat(pieces, down, pieces // 2)
    ahead[0].wait_recv()
    peer_g.start()
    repeat(pieces, functools.partial(with_sibling, 0))
    for k in range(1, SIDE):
        s_copy(0, k).start()

    def backward(which):
        at = pl.ds(at_multiple(which * half, half), half)
        act_grad = lax.dot_general(
            gc[at, :], wd[...], (((1,), (1,)), ((), ())), preferred_element_type=F32
        )
        g_val, u_val = gate[at, :], up[at, :]
        sig = jax.nn.sigmoid(g_val)
        gb[at, :] = (act_grad * u_val * sig * (1.0 + g_val * (1.0 - sig))).astype(BF16)
        ub[at, :] = (act_grad * (g_val * sig)).astype(BF16)

    repeat(2, backward)
    peer_g.near()
    loads[4].wait()
    loads[5].wait()

    def columns(piece):
        at = piece_at(piece)
        turned = xc[:, at].T
        mg[at, :] = advance(
            wg[at, :], mg[at, :], jnp.dot(turned, gb[...], preferred_element_type=F32)
        )
        gossip(1, piece).start()
        mu[at, :] = advance(
            wu[at, :], mu[at, :], jnp.dot(turned, ub[...], preferred_element_type=F32)
        )
        gossip(2, piece).start()

    repeat(pieces, columns)
    peer_g.spread()

    for one in g_waves:
        one.sent()
        one.sent_blocks()
    repeat(pieces, functools.partial(for_sibling, 1))
    peer_g.onward()
    repeat(pieces, functools.partial(with_sibling, 1))
    for k in range(1, SIDE):
        s_copy(1, k).start()
    peer_g.last()
    along_s(0)

    peer_g.other()
    repack(gp3, gc, 0, blocks, pl.ds(0, depth))
    ahead[1].wait_recv()
    ahead[2].wait_recv()

    def peer_rows(piece):
        at = piece_at(piece)
        grad = jnp.dot(actp[rows_early, :], gc[:, at], preferred_element_type=F32)
        theirs = (rd[rows_early, at].astype(F32) - LEARN * grad).astype(BF16)
        both = md[rows_early, at].astype(F32) + theirs.astype(F32)
        nd_o[0, rows_early, at] = (both * 0.5).astype(BF16)

    repeat(pieces, peer_rows)
    along_s(1)

    repeat(pieces, functools.partial(finish, 0))

    def finish_both(piece):
        finish(1, piece)
        finish(2, piece)

    repeat(pieces - 3, finish_both)
    for kind in (0, 1):
        total(kind)
    repeat(pieces, finish_both, pieces - 3)

    peer_g.sent()
    peer_g.sent_groups()
    for kind in (0, 1):
        repeat(pieces, lambda piece: pair_copy(kind, piece).wait_send())
        for k in range(1, SIDE):
            s_copy(kind, k).wait_send()
            f_copy(kind, k).wait_send()
    for copy in ahead:
        copy.wait_send()
    for kind in range(3):
        repeat(pieces, lambda piece: gossip(kind, piece).wait_send())


def call(level, *args):
    x_in, _, wg, _, wd = args[:5]
    rows, depth = x_in.shape
    width = wg.shape[2]
    blocks = SIDE * SIDE
    tokens = 2 * blocks * rows
    pieces = depth // CHUNK
    any_space = pl.BlockSpec(memory_space=pl.ANY)
    vmem = pl.BlockSpec(memory_space=pltpu.VMEM)
    dma = pltpu.SemaphoreType.DMA
    tall, flat = pltpu.VMEM((depth, width), BF16), pltpu.VMEM((width, depth), BF16)
    return pl.pallas_call(
        functools.partial(kernel, level),
        name="step_level_" + str(level),
        out_shape=(
            jax.ShapeDtypeStruct((rows, depth), BF16),
            jax.ShapeDtypeStruct((rows, depth), BF16),
            jax.ShapeDtypeStruct(wg.shape, BF16),
            jax.ShapeDtypeStruct(wg.shape, BF16),
            jax.ShapeDtypeStruct(wd.shape, BF16),
        ),
        in_specs=[any_space] * 8,
        out_specs=(vmem,) * 5,
        scratch_shapes=[
            pltpu.VMEM((2 * blocks, rows, depth), BF16),
            pltpu.VMEM((2 * blocks, rows, depth), BF16),
            pltpu.VMEM((tokens, depth), BF16),
            pltpu.VMEM((tokens, depth), BF16),
            tall,
            tall,
            flat,
            tall,
            tall,
            flat,
            tall,
            tall,
            flat,
            pltpu.VMEM((tokens, width), F32),
            pltpu.VMEM((tokens, width), F32),
            pltpu.VMEM((tokens, width), BF16),
            pltpu.VMEM((tokens, width), BF16),
            pltpu.VMEM((tokens, width), BF16),
            pltpu.VMEM((width, tokens), BF16),
            pltpu.VMEM((max(EARLY), depth), BF16),
            pltpu.VMEM((2 * blocks, rows, depth), BF16),
            pltpu.VMEM((max(EARLY), tokens), BF16),
            pltpu.VMEM((blocks, rows, depth), BF16),
            pltpu.VMEM((blocks, rows, depth), BF16),
            pltpu.VMEM((blocks, rows, depth), BF16),
            pltpu.VMEM((blocks, rows, depth), BF16),
            pltpu.VMEM((rows, depth), BF16),
            pltpu.VMEM((rows, depth), BF16),
            dma((8,)),
            dma((3,)),
            dma((4, 24)),
            dma((4, 24)),
            dma((2, pieces)),
            dma((2, pieces)),
            dma((2, 2 * SIDE)),
            dma((2, 2 * SIDE)),
            dma((3 * pieces + 3,)),
            dma((3 * pieces + 3,)),
        ],
        compiler_params=pltpu.CompilerParams(
            collective_id=level, has_side_effects=True, vmem_limit_bytes=57 << 20
        ),
    )(*args)


def store_kernel(*refs):
    count = len(refs) // 2
    sem = refs[-1]
    copies = [
        pltpu.make_async_copy(refs[i], refs[count + i], sem.at[i]) for i in range(count)
    ]
    for copy in copies:
        copy.start()
    for copy in copies:
        copy.wait()


def store(*arrays):
    return pl.pallas_call(
        store_kernel,
        name="store",
        out_shape=tuple(jax.ShapeDtypeStruct(a.shape, a.dtype) for a in arrays),
        in_specs=[pl.BlockSpec(memory_space=pltpu.VMEM)] * len(arrays),
        out_specs=(pl.BlockSpec(memory_space=pl.ANY),) * len(arrays),
        scratch_shapes=[pltpu.SemaphoreType.DMA((len(arrays),))],
    )(*arrays)


def per_device(*args):
    *arrays, step_count = args
    levels = (lax.axis_size("rep") // SPLIT).bit_length() - 1
    results = lax.switch(
        jnp.mod(step_count, levels),
        [functools.partial(call, level) for level in range(levels)],
        *arrays,
    )
    return store(*results)


def solution(mesh):
    rows, columns, across = P(("rep", "tp"), None), P("rep", None, "tp"), P("rep", "tp", None)
    return jax.shard_map(
        per_device,
        mesh=mesh,
        in_specs=(rows, rows, columns, columns, across, columns, columns, across, P()),
        out_specs=(rows, rows, columns, columns, across),
        check_vma=False,
    )
```

```python
import functools

import jax
import jax.numpy as jnp
from jax import lax
from jax.experimental import pallas as pl
from jax.experimental.pallas import tpu as pltpu
from jax.sharding import PartitionSpec as P

MESH = pl.DeviceIdType.MESH
SPLIT = 4
SIDE = 4
MOMENT = 0.9
LEARN = 0.001
CHUNK = 512
FINE = 256
EARLY = (192, 96, 96)
F32 = jnp.float32
BF16 = jnp.bfloat16


def at_multiple(index, of):
    return pl.multiple_of(index, of)


def kernel(
    level,
    x_in,
    g_in,
    wg_in,
    wu_in,
    wd_in,
    mg_in,
    mu_in,
    md_in,
    out_o,
    gin_o,
    ng_o,
    nu_o,
    nd_o,
    x3,
    g3,
    xc,
    gc,
    wg,
    wu,
    wd,
    mg,
    mu,
    md,
    rg,
    ru,
    rd,
    gate,
    up,
    act,
    gb,
    ub,
    actt,
    he,
    gp3,
    actp,
    sx,
    sg,
    px,
    pg,
    xo,
    go,
    load_sem,
    own_sem,
    wave_send,
    wave_recv,
    pair_send,
    pair_recv,
    sum_send,
    sum_recv,
    gossip_send,
    gossip_recv,
):
    rows, depth = x_in.shape
    width = wg.shape[1]
    blocks = SIDE * SIDE
    half = blocks * rows
    r, t = lax.axis_index("rep"), lax.axis_index("tp")
    z, core = r // SPLIT, r % 2
    x, y = (r // 2) % 2 * 2 + t // SIDE, t % SIDE
    s = x + core * (y - x)
    f = y + core * (x - y)

    def turn(index):
        return (index + SIDE) % SIDE

    def device(cc, ss, ff, zz=None):
        xx = ss + cc * (ff - ss)
        yy = ff + cc * (ss - ff)
        return ((z if zz is None else zz) * SPLIT + xx // 2 * 2 + cc, xx % 2 * SIDE + yy)

    f_plus, f_minus = device(core, s, turn(f + 1)), device(core, s, turn(f - 1))
    s_plus, s_minus = device(core, turn(s + 1), f), device(core, turn(s - 1), f)
    sibling = (z * SPLIT + x // 2 * 2 + 1 - core, t)
    step = 2**level
    partner_z = z + step - 2 * step * (z // step % 2)
    partner = device(core, s, f, partner_z)
    s_peers = [device(core, turn(s + k), f) for k in range(1, SIDE)]
    f_peers = [device(core, s, turn(f + k)) for k in range(1, SIDE)]

    def remote(src, dst, send, recv, to):
        return pltpu.make_async_remote_copy(
            src_ref=src, dst_ref=dst, send_sem=send, recv_sem=recv, device_id=to, device_id_type=MESH
        )

    loads = [
        pltpu.make_async_copy(src.at[0], dst, load_sem.at[i])
        for i, (src, dst) in enumerate(
            ((wd_in, wd), (md_in, md), (wg_in, wg), (wu_in, wu), (mg_in, mg), (mu_in, mu))
        )
    ]
    loads += [
        pltpu.make_async_copy(src, dst, load_sem.at[6 + i])
        for i, (src, dst) in enumerate(((x_in, xo), (g_in, go)))
    ]
    pieces = depth // CHUNK

    def when(condition, run):
        if isinstance(condition, bool):
            if condition:
                run()
        else:
            pl.when(condition)(run)

    class Wave:
        def __init__(self, w, src, land, col, wide):
            self.w, self.src, self.land, self.col, self.wide = w, src, land, col, wide

        def cols(self, part):
            wide = self.wide
            if part == "all":
                return pl.ds(self.col, wide)
            return pl.ds(self.col + (wide // 2 if part == "high" else 0), wide // 2)

        def block(self, ds, df, part="all"):
            at = core * blocks + turn(s + ds) * SIDE + turn(f + df)
            return self.land.at[at, :, self.cols(part)]

        def group(self, ds, part="all", other=False):
            if other:
                at = (1 - core) * blocks + turn(f + ds) * SIDE
            else:
                at = core * blocks + turn(s + ds) * SIDE
            return self.land.at[pl.ds(at, SIDE), :, self.cols(part)]

        def copy(self, src, dst, slot, to):
            return remote(src, dst, wave_send.at[self.w, slot], wave_recv.at[self.w, slot], to)

        def send(self, src, dst, slot, to):
            self.copy(src, dst, slot, to).start()

        def wait(self, dst, slot):
            self.copy(dst, dst, slot, sibling).wait_recv()

        def own(self):
            return pltpu.make_async_copy(
                self.src.at[:, self.cols("all")], self.block(0, 0), own_sem.at[self.w]
            )

        def start(self):
            to = self.block(0, 0)
            mine = to if self.src is None else self.src.at[:, self.cols("all")]
            self.send(mine, to, 0, f_plus)
            self.send(mine, to, 1, f_minus)
            if self.src is not None:
                self.own().start()

        def near(self):
            self.wait(self.block(0, -1), 0)
            self.wait(self.block(0, 1), 1)
            for df, part, slot, to in ((-1, "low", 2, f_plus), (1, "high", 3, f_minus)):
                ref = self.block(0, df, part)
                self.send(ref, ref, slot, to)

        def far(self):
            self.wait(self.block(0, 2, "low"), 2)
            self.wait(self.block(0, 2, "high"), 3)

        def to_sibling(self, ds, slot):
            ref = self.group(ds)
            self.send(ref, ref, 20 + slot, sibling)

        def spread(self):
            self.far()
            if self.src is not None:
                self.own().wait()
            ref = self.group(0)
            self.send(ref, ref, 4, s_plus)
            self.send(ref, ref, 8, s_minus)
            self.to_sibling(0, 0)

        def onward(self):
            for ds, part, slot, to in ((-1, "low", 4, s_plus), (1, "high", 8, s_minus)):
                self.wait(self.group(ds), slot)
                ref = self.group(ds, part)
                self.send(ref, ref, slot + 8, to)
            self.to_sibling(-1, 1)
            self.to_sibling(1, 2)

        def last(self):
            self.wait(self.group(2, "low"), 12)
            self.wait(self.group(2, "high"), 16)
            self.to_sibling(2, 3)

        def other(self):
            for slot, ds in enumerate((0, -1, 1, 2)):
                self.wait(self.group(ds, other=True), 20 + slot)

        def sent(self):
            for slot in (0, 1):
                self.copy(self.block(0, 0), self.block(0, 0), slot, sibling).wait_send()
            for slot, part in ((2, "low"), (3, "high")):
                self.copy(self.block(0, 0, part), self.block(0, 0, part), slot, sibling).wait_send()
            for slot in (20, 21, 22, 23):
                self.copy(self.group(0), self.group(0), slot, sibling).wait_send()

        def sent_groups(self):
            for slot, part in ((4, "all"), (8, "all"), (12, "low"), (16, "high")):
                self.copy(self.group(0, part), self.group(0, part), slot, sibling).wait_send()

        def step(self, n):
            if n == 0:
                self.start()
                self.spread_block(0, self.src.at[:, self.cols("all")])
            elif n == 1:
                self.near()
                self.spread_block(-1)
                self.spread_block(1)
                self.onward_block(0)
            elif n == 2:
                self.far()
                self.spread_block(2)
                self.own().wait()
                self.to_sibling(0, 0)
                self.onward_block(-1)
                self.onward_block(1)
            elif n == 3:
                self.onward_block(2)
                self.to_sibling(-1, 1)
                self.to_sibling(1, 2)
            elif n == 4:
                for df in (0, -1, 1, 2):
                    self.last_block(df)
                self.to_sibling(2, 3)
            else:
                self.other()

        def spread_block(self, df, src=None):
            ref = self.block(0, df)
            src = ref if src is None else src
            self.send(src, ref, 4 + df % SIDE, s_plus)
            self.send(src, ref, 8 + df % SIDE, s_minus)

        def onward_block(self, df):
            for ds, part, slot, to in ((-1, "low", 4, s_plus), (1, "high", 8, s_minus)):
                self.wait(self.block(ds, df), slot + df % SIDE)
                ref = self.block(ds, df, part)
                self.send(ref, ref, slot + 8 + df % SIDE, to)

        def last_block(self, df):
            self.wait(self.block(2, df, "low"), 12 + df % SIDE)
            self.wait(self.block(2, df, "high"), 16 + df % SIDE)

        def sent_blocks(self):
            for slot, part in ((4, "all"), (8, "all"), (12, "low"), (16, "high")):
                for df in range(SIDE):
                    ref = self.block(0, 0, part)
                    self.copy(ref, ref, slot + df, sibling).wait_send()

    first = Wave(0, x_in, x3, 0, depth)
    g_waves = [Wave(1 + i, g_in, g3, i * depth // 2, depth // 2) for i in (0, 1)]
    peer_g = Wave(3, None, gp3, 0, depth)

    def piece_at(piece):
        return pl.ds(
            piece * CHUNK if isinstance(piece, int) else at_multiple(piece * CHUNK, CHUNK), CHUNK
        )

    def fine_at(piece):
        return pl.ds(at_multiple(piece * FINE, FINE), FINE)

    fines, ratio = depth // FINE, CHUNK // FINE

    def repack(land, flat, start, pairs, cols):
        def body(i, carry):
            b = start + 2 * i
            pair = jnp.concatenate(
                [land[b, :, cols].astype(F32), land[b + 1, :, cols].astype(F32)], 0
            )
            flat[pl.ds(at_multiple(b * rows, 2 * rows), 2 * rows), cols] = pair.astype(BF16)
            return carry

        lax.fori_loop(0, pairs, body, 0)

    def forward(which):
        at = pl.ds(at_multiple(which * half, half), half)
        tokens = xc[at, :]
        g_val = jnp.dot(tokens, wg[...], preferred_element_type=F32)
        gate[at, :] = g_val
        u_val = jnp.dot(tokens, wu[...], preferred_element_type=F32)
        up[at, :] = u_val
        act[at, :] = (g_val * jax.nn.sigmoid(g_val) * u_val).astype(BF16)

    def advance(weight, moment, grad):
        total = MOMENT * moment.astype(F32) + grad
        return (weight.astype(F32) - LEARN * total).astype(BF16)

    weights = ((md, rd, nd_o), (mg, rg, ng_o), (mu, ru, nu_o))
    early = EARLY[level]
    rows_early = pl.ds(0, early)
    mine_at = core * blocks + s * SIDE + f
    ahead = [
        remote(src, dst, gossip_send.at[3 * pieces + i], gossip_recv.at[3 * pieces + i], partner)
        for i, (src, dst) in enumerate(
            (
                (g_in, gp3.at[mine_at]),
                (he.at[rows_early], rd.at[rows_early]),
                (actt.at[rows_early], actp.at[rows_early]),
            )
        )
    ]

    def index_of(kind, at):
        if kind == 0:
            return (pl.ds(early, width - early), at)
        return (at, slice(None))

    def gossip(kind, piece):
        mine, theirs, _ = weights[kind]
        index = index_of(kind, piece_at(piece))
        n = kind * pieces + piece
        return remote(
            mine.at[index], theirs.at[index], gossip_send.at[n], gossip_recv.at[n], partner
        )

    def gossip_start(kind, piece):
        gossip(kind, piece).start()

    def finish(kind, piece):
        mine, theirs, to = weights[kind]
        gossip(kind, piece).wait_recv()

        def fine(i):
            index = index_of(kind, fine_at(piece * ratio + i))
            both = mine[index].astype(F32) + theirs[index].astype(F32)
            to[(0, *index)] = (both * 0.5).astype(BF16)

        repeat(ratio, fine)

    def repeat(count, run, start=0):
        def body(i, carry):
            run(i)
            return carry

        lax.fori_loop(start, count, body, 0)

    def partial(kind, which, at):
        part = pl.ds(at_multiple(which * half, half), half)
        if kind == 0:
            return jnp.dot(act[part, :], wd[:, at], preferred_element_type=F32)
        nt = (((1,), (1,)), ((), ()))
        return lax.dot_general(
            gb[part, :], wg[at, :], nt, preferred_element_type=F32
        ) + lax.dot_general(ub[part, :], wu[at, :], nt, preferred_element_type=F32)

    sums = ((x3, sx, px, out_o), (g3, sg, pg, gin_o))
    given = (xo, go)

    def pair_copy(kind, piece):
        stage, theirs, _, _ = sums[kind]
        at = fine_at(piece)
        return remote(
            stage.at[pl.ds((1 - core) * blocks, blocks), :, at],
            theirs.at[:, :, at],
            pair_send.at[kind, piece],
            pair_recv.at[kind, piece],
            sibling,
        )

    def s_copy(kind, k):
        stage, _, theirs, _ = sums[kind]
        return remote(
            stage.at[pl.ds(core * blocks + turn(s + k) * SIDE, SIDE)],
            theirs.at[pl.ds(k * SIDE, SIDE)],
            sum_send.at[kind, k],
            sum_recv.at[kind, k],
            s_peers[k - 1],
        )

    def f_copy(kind, k):
        stage, _, theirs, _ = sums[kind]
        return remote(
            stage.at[core * blocks + s * SIDE + turn(f + k)],
            theirs.at[k],
            sum_send.at[kind, SIDE + k],
            sum_recv.at[kind, SIDE + k],
            f_peers[k - 1],
        )

    def for_sibling(kind, piece):
        stage = sums[kind][0]
        at = fine_at(piece)
        value = partial(kind, 1 - core, at)
        for i in range(blocks):
            stage[(1 - core) * blocks + i, :, at] = value[i * rows : (i + 1) * rows].astype(BF16)
        pair_copy(kind, piece).start()

    def with_sibling(kind, piece):
        stage, theirs, _, _ = sums[kind]
        at = fine_at(piece)
        value = partial(kind, core, at)
        pair_copy(kind, piece).wait_recv()
        for i in range(blocks):
            stage[core * blocks + i, :, at] = (
                value[i * rows : (i + 1) * rows] + theirs[i, :, at].astype(F32)
            ).astype(BF16)

    def along_s(kind):
        stage, _, theirs, _ = sums[kind]
        for k in range(1, SIDE):
            s_copy(kind, k).wait_recv()

        def add(i):
            b = core * blocks + s * SIDE + i
            value = stage[b].astype(F32)
            for k in range(1, SIDE):
                value = value + theirs[k * SIDE + i].astype(F32)
            stage[b] = value.astype(BF16)

        repeat(SIDE, add)
        for k in range(1, SIDE):
            f_copy(kind, k).start()

    def total(kind):
        stage, _, theirs, to = sums[kind]
        for k in range(1, SIDE):
            f_copy(kind, k).wait_recv()
        value = stage[mine_at].astype(F32)
        for k in range(1, SIDE):
            value = value + theirs[k].astype(F32)
        loads[6 + kind].wait()
        to[...] = (given[kind][...].astype(F32) + value).astype(BF16)

    for load in loads:
        load.start()
    barrier = pltpu.get_barrier_semaphore()
    greeted = s_peers + f_peers + [sibling, partner]
    for to in greeted:
        pl.semaphore_signal(barrier, inc=1, device_id=to, device_id_type=MESH)
    pl.semaphore_wait(barrier, len(greeted))

    first.step(0)
    ahead[0].start()
    loads[0].wait()
    loads[1].wait()

    def decayed(piece):
        at = piece_at(piece)
        he[rows_early, at] = advance(wd[rows_early, at], md[rows_early, at], 0.0)

    repeat(pieces, decayed)
    ahead[1].start()
    first.step(1)
    first.step(2)
    g_waves[0].step(0)
    first.step(3)
    g_waves[0].step(1)
    g_waves[1].step(0)

    def token_half(i):
        def own_half():
            first.step(4)
            loads[2].wait()
            loads[3].wait()

        def other_half():
            g_waves[0].step(2)
            g_waves[1].step(1)
            first.step(5)

        when(i == 0, own_half)
        when(i == 1, other_half)
        which = core + i * (1 - 2 * core)
        repack(x3, xc, which * blocks, blocks // 2, pl.ds(0, depth))
        forward(which)

    repeat(2, token_half)
    g_waves[0].step(3)
    g_waves[1].step(2)
    actt[...] = act[...].T
    ahead[2].start()
    g_waves[0].step(4)
    g_waves[1].step(3)

    def down(piece):
        def fine(i):
            at = fine_at(piece * ratio + i)
            grad = jnp.dot(actt[...], gc[:, at], preferred_element_type=F32)
            md[:, at] = advance(wd[:, at], md[:, at], grad)

        repeat(ratio, fine)
        gossip(0, piece).start()

    g_waves[0].step(5)
    repack(g3, gc, 0, blocks, pl.ds(0, depth // 2))
    repeat(pieces // 2, down)
    first.sent()
    first.sent_blocks()
    g_waves[1].step(4)
    repeat(fines, functools.partial(for_sibling, 0))
    g_waves[1].step(5)
    repack(g3, gc, 0, blocks, pl.ds(depth // 2, depth // 2))
    repeat(pieces, down, pieces // 2)
    ahead[0].wait_recv()
    peer_g.start()
    repeat(fines, functools.partial(with_sibling, 0))
    for k in range(1, SIDE):
        s_copy(0, k).start()

    def backward(which):
        at = pl.ds(at_multiple(which * half // 2, half // 2), half // 2)
        act_grad = lax.dot_general(
            gc[at, :], wd[...], (((1,), (1,)), ((), ())), preferred_element_type=F32
        )
        g_val, u_val = gate[at, :], up[at, :]
        sig = jax.nn.sigmoid(g_val)
        gb[at, :] = (act_grad * u_val * sig * (1.0 + g_val * (1.0 - sig))).astype(BF16)
        ub[at, :] = (act_grad * (g_val * sig)).astype(BF16)

    repeat(4, backward)
    peer_g.near()
    loads[4].wait()
    loads[5].wait()

    def columns(piece):
        def fine(i):
            at = fine_at(piece * ratio + i)
            turned = xc[:, at].T
            for weight, moment, back in ((wg, mg, gb), (wu, mu, ub)):
                grad = jnp.dot(turned, back[...], preferred_element_type=F32)
                moment[at, :] = advance(weight[at, :], moment[at, :], grad)

        repeat(ratio, fine)
        gossip(1, piece).start()
        gossip(2, piece).start()

    repeat(pieces, columns)
    peer_g.spread()

    for one in g_waves:
        one.sent()
        one.sent_blocks()
    repeat(fines, functools.partial(for_sibling, 1))
    peer_g.onward()
    repeat(fines, functools.partial(with_sibling, 1))
    for k in range(1, SIDE):
        s_copy(1, k).start()
    peer_g.last()
    along_s(0)

    peer_g.other()
    repack(gp3, gc, 0, blocks, pl.ds(0, depth))
    ahead[1].wait_recv()
    ahead[2].wait_recv()

    def peer_rows(piece):
        at = fine_at(piece)
        grad = jnp.dot(actp[rows_early, :], gc[:, at], preferred_element_type=F32)
        theirs = (rd[rows_early, at].astype(F32) - LEARN * grad).astype(BF16)
        both = md[rows_early, at].astype(F32) + theirs.astype(F32)
        nd_o[0, rows_early, at] = (both * 0.5).astype(BF16)

    repeat(fines, peer_rows)
    along_s(1)

    repeat(pieces, functools.partial(finish, 0))

    def finish_both(piece):
        finish(1, piece)
        finish(2, piece)

    repeat(pieces - 3, finish_both)
    for kind in (0, 1):
        total(kind)
    repeat(pieces, finish_both, pieces - 3)

    peer_g.sent()
    peer_g.sent_groups()
    for kind in (0, 1):
        repeat(fines, lambda piece: pair_copy(kind, piece).wait_send())
        for k in range(1, SIDE):
            s_copy(kind, k).wait_send()
            f_copy(kind, k).wait_send()
    for copy in ahead:
        copy.wait_send()
    for kind in range(3):
        repeat(pieces, lambda piece: gossip(kind, piece).wait_send())


def call(level, *args):
    x_in, _, wg, _, wd = args[:5]
    rows, depth = x_in.shape
    width = wg.shape[2]
    blocks = SIDE * SIDE
    tokens = 2 * blocks * rows
    pieces = depth // CHUNK
    any_space = pl.BlockSpec(memory_space=pl.ANY)
    vmem = pl.BlockSpec(memory_space=pltpu.VMEM)
    dma = pltpu.SemaphoreType.DMA
    tall, flat = pltpu.VMEM((depth, width), BF16), pltpu.VMEM((width, depth), BF16)
    return pl.pallas_call(
        functools.partial(kernel, level),
        name="step_level_" + str(level),
        out_shape=(
            jax.ShapeDtypeStruct((rows, depth), BF16),
            jax.ShapeDtypeStruct((rows, depth), BF16),
            jax.ShapeDtypeStruct(wg.shape, BF16),
            jax.ShapeDtypeStruct(wg.shape, BF16),
            jax.ShapeDtypeStruct(wd.shape, BF16),
        ),
        in_specs=[any_space] * 8,
        out_specs=(vmem,) * 5,
        scratch_shapes=[
            pltpu.VMEM((2 * blocks, rows, depth), BF16),
            pltpu.VMEM((2 * blocks, rows, depth), BF16),
            pltpu.VMEM((tokens, depth), BF16),
            pltpu.VMEM((tokens, depth), BF16),
            tall,
            tall,
            flat,
            tall,
            tall,
            flat,
            tall,
            tall,
            flat,
            pltpu.VMEM((tokens, width), F32),
            pltpu.VMEM((tokens, width), F32),
            pltpu.VMEM((tokens, width), BF16),
            pltpu.VMEM((tokens, width), BF16),
            pltpu.VMEM((tokens, width), BF16),
            pltpu.VMEM((width, tokens), BF16),
            pltpu.VMEM((max(EARLY), depth), BF16),
            pltpu.VMEM((2 * blocks, rows, depth), BF16),
            pltpu.VMEM((max(EARLY), tokens), BF16),
            pltpu.VMEM((blocks, rows, depth), BF16),
            pltpu.VMEM((blocks, rows, depth), BF16),
            pltpu.VMEM((blocks, rows, depth), BF16),
            pltpu.VMEM((blocks, rows, depth), BF16),
            pltpu.VMEM((rows, depth), BF16),
            pltpu.VMEM((rows, depth), BF16),
            dma((8,)),
            dma((3,)),
            dma((4, 24)),
            dma((4, 24)),
            dma((2, depth // FINE)),
            dma((2, depth // FINE)),
            dma((2, 2 * SIDE)),
            dma((2, 2 * SIDE)),
            dma((3 * pieces + 3,)),
            dma((3 * pieces + 3,)),
        ],
        compiler_params=pltpu.CompilerParams(
            collective_id=level, has_side_effects=True, vmem_limit_bytes=57 << 20
        ),
    )(*args)


def store_kernel(*refs):
    count = len(refs) // 2
    sem = refs[-1]
    copies = [
        pltpu.make_async_copy(refs[i], refs[count + i], sem.at[i]) for i in range(count)
    ]
    for copy in copies:
        copy.start()
    for copy in copies:
        copy.wait()


def store(*arrays):
    return pl.pallas_call(
        store_kernel,
        name="store",
        out_shape=tuple(jax.ShapeDtypeStruct(a.shape, a.dtype) for a in arrays),
        in_specs=[pl.BlockSpec(memory_space=pltpu.VMEM)] * len(arrays),
        out_specs=(pl.BlockSpec(memory_space=pl.ANY),) * len(arrays),
        scratch_shapes=[pltpu.SemaphoreType.DMA((len(arrays),))],
    )(*arrays)


def per_device(*args):
    *arrays, step_count = args
    levels = (lax.axis_size("rep") // SPLIT).bit_length() - 1
    results = lax.switch(
        jnp.mod(step_count, levels),
        [functools.partial(call, level) for level in range(levels)],
        *arrays,
    )
    return store(*results)


def solution(mesh):
    rows, columns, across = P(("rep", "tp"), None), P("rep", None, "tp"), P("rep", "tp", None)
    return jax.shard_map(
        per_device,
        mesh=mesh,
        in_specs=(rows, rows, columns, columns, across, columns, columns, across, P()),
        out_specs=(rows, rows, columns, columns, across),
        check_vma=False,
    )
```
